32 devices in a mesh: groups: 2 (over x), tensor: 16 (over z, y, core).
Axes of the slice: x: 2, y: 2, z: 4, core: 2. Of those that a mesh axis runs over, the one named last changes fastest.
Arguments:
- tokens: bfloat16 [1024, 8192], P(('groups', 'tensor')), parts along dimension 0, may hold values from -6 to 6
- attn_gain: float32 [8192], replicated, may hold values from 0.6 to 10, as said below
- w_query: bfloat16 [8192, 8192], P(None, 'tensor'), may hold values from -0.0625 to 0.0625
- w_key: bfloat16 [8192, 1024], P(None, 'tensor'), may hold values from -0.0625 to 0.0625
- w_value: bfloat16 [8192, 1024], P(None, 'tensor'), may hold values from -0.0625 to 0.0625
- w_output: bfloat16 [8192, 8192], P('tensor'), may hold values from -0.0625 to 0.0625
- doc_ids: int32 [1024], P('groups'), parts along dimension 0, may hold values from 0 to 3, never falling along the last dimension, each value on 1 to 256 neighbouring positions
Outputs:
- attention: bfloat16 [1024, 8192], P(('groups', 'tensor')), parts along dimension 0
- hidden: bfloat16 [1024, 8192], P(('groups', 'tensor')), parts along dimension 0
The draws below stay inside these ranges and needn't reach their ends.
There are 2 independent parts, one for each index of `groups`. The reference program is written for one: setup_inputs(seed, part) draws one part's arguments, and reference() takes and returns one part's arrays. A program takes and returns all parts, laid end to end along the dimension named above; an argument that names none is the same for every part. Nothing has to cross between parts.
Inputs may be any that keep to these rules, and one draw needn't show every extreme that they name: `doc_ids`: document numbers never fall along the block, each document has 1 to 256 tokens and one has exactly that many. `attn_gain`: positive gains.
All inputs are finite; a program needn't handle non-finite values.
Results may differ from the reference program's by a relative error of at most 0.015.
The reference program's roundings to bfloat16 on the way (of `normed`, `queries`, `key_raw`, `keys`, `probs` and `attended`) count: a program that leaves them out, or rounds other values in their place, can miss the bound.
Values may be sent and summed in bfloat16 or wider, within the bound.
A program may use at most 128 MiB of HBM per device.

```python
import math
import jax
import jax.numpy as jnp
import numpy as np
from jax import lax

D = 8192
HEADS = 64
KV_HEADS = 8
HEAD_DIM = 128
TOKENS = 512
N_TENSOR = 16


def draw_attn_gain(key, part):
    key = jax.random.fold_in(key, 7)
    gains = jax.random.uniform(key, (D,), jnp.float32, 0.6, 1.4)
    return gains


def shard_levels(own_key, shape, pieces, smallest, top_value):
    gain = 1.0
    for dim, shards_of in pieces:
        draws = jax.random.uniform(jax.random.fold_in(jax.random.fold_in(own_key, 6), dim), (shards_of,), jnp.float32, smallest / len(pieces), top_value / len(pieces))
        gain = gain * jnp.repeat(jnp.exp(draws), shape[dim] // shards_of).reshape((-1,) + (1,) * (len(shape) - 1 - dim))
    return gain


def profile(count, total, reach, skew):
    portions = [(1 << 20) // math.isqrt(grade ** skew) + 1 for grade in range(2, count + 1)]
    surplus, holding = total - reach - (count - 1), [1] * (count - 1)
    while surplus > 0:
        free = [i for i in range(count - 1) if holding[i] < reach]
        pool, budget = sum([portions[i] for i in free]), surplus
        for i in free:
            addition = min(reach - holding[i], max(1, budget * portions[i] // pool), surplus)
            holding[i] = holding[i] + addition
            surplus = surplus - addition
    return np.array([reach] + holding)


def uneven_parts(stream_key, number_of, total, bound, lean):
    if number_of == 2:
        one = jax.random.randint(stream_key, (), max(1, total - bound), min(bound, total - 1) + 1)
        return jnp.stack([one, total - one])
    lengths = jnp.asarray(profile(number_of, total, bound, lean), jnp.int32)
    couples = (number_of - 1) // 2
    donor, sink = lengths[1:1 + 2 * couples:2], lengths[2:2 + 2 * couples:2]
    room = jnp.minimum(donor - 1, bound - sink)
    shifted = jax.random.randint(jax.random.fold_in(stream_key, 1), (couples,), 0, 1 << 20) % (room + 1)
    lengths = lengths.at[1:1 + 2 * couples:2].set(donor - shifted).at[2:2 + 2 * couples:2].set(sink + shifted)
    return lengths[jax.random.permutation(jax.random.fold_in(stream_key, 2), number_of)]


def bell_draw(rng, dims, spread, bound, shards=(), kind=jnp.bfloat16):
    drawn = jax.random.normal(rng, dims, jnp.float32) * spread
    if len(shards) > 0:
        drawn = shard_levels(rng, dims, shards, -0.22, 0.18) * drawn
    return jnp.clip(drawn, min=-bound, max=bound).astype(kind)


def setup_inputs(seed: int = 0, part: int = 0) -> dict:
    streams_of = jax.random.split(jax.random.key(seed), 8)
    part_splits = jax.random.split(jax.random.fold_in(streams_of[7], part), 8)
    return {
        "tokens": bell_draw(part_splits[0], (TOKENS, D), 1.0, 6.0, ((0, 16),)),
        "attn_gain": draw_attn_gain(jax.random.fold_in(streams_of[7], 71), part),
        "w_query": bell_draw(streams_of[2], (D, HEADS * HEAD_DIM), D ** -0.5, 0.0625, ((1, 16),)),
        "w_key": bell_draw(streams_of[3], (D, KV_HEADS * HEAD_DIM), D ** -0.5, 0.0625, ((1, 16),)),
        "w_value": bell_draw(streams_of[4], (D, KV_HEADS * HEAD_DIM), D ** -0.5, 0.0625, ((1, 16),)),
        "w_output": bell_draw(streams_of[5], (HEADS * HEAD_DIM, D), (HEADS * HEAD_DIM) ** -0.5, 0.0625, ((0, 16),)),
        "doc_ids": jnp.searchsorted(jnp.cumsum(uneven_parts(part_splits[6], 4, TOKENS, TOKENS // 2, 1)), jnp.arange(TOKENS), side="right").astype(jnp.int32),
    }


def rotary_angles(doc_ids, head_dim):
    count = doc_ids.shape[0]
    first = lax.optimization_barrier(jnp.sum((doc_ids[None, :] < doc_ids[:, None]).astype(jnp.int32), axis=1))
    position = (jnp.arange(count, dtype=jnp.int32) - first).astype(jnp.float32)
    freq = jnp.float32(500000.0) ** (-(jnp.arange(head_dim // 2, dtype=jnp.float32) * 2.0 / head_dim))
    angle = position[:, None] * freq[None, :]
    return (jnp.cos(angle)[:, None, :], jnp.sin(angle)[:, None, :])

def apply_rope(vectors, cosine, sine):
    half = vectors.shape[-1] // 2
    first_half = vectors[..., :half]
    second_half = vectors[..., half:]
    return jnp.concatenate([first_half * cosine - second_half * sine, second_half * cosine + first_half * sine], axis=-1)

def reference(tokens, attn_gain, w_query, w_key, w_value, w_output, doc_ids):
    rows = tokens.astype(jnp.float32)
    normed = (rows * lax.rsqrt(lax.optimization_barrier(jnp.mean(rows * rows, axis=-1, keepdims=True)) + 1e-05) * attn_gain).astype(jnp.bfloat16)
    count = rows.shape[0]
    cosine, sine = rotary_angles(doc_ids, HEAD_DIM)
    query_raw = jnp.dot(normed, w_query, preferred_element_type=jnp.float32).reshape(count, HEADS, HEAD_DIM)
    queries = apply_rope(query_raw, cosine, sine).astype(jnp.bfloat16)
    key_raw = jnp.dot(normed, w_key, preferred_element_type=jnp.float32).astype(jnp.bfloat16)
    values = jnp.dot(normed, w_value, preferred_element_type=jnp.float32).astype(jnp.bfloat16).reshape(count, KV_HEADS, HEAD_DIM)
    keys = apply_rope(key_raw.astype(jnp.float32).reshape(count, KV_HEADS, HEAD_DIM), cosine, sine).astype(jnp.bfloat16)
    index = jnp.arange(count, dtype=jnp.int32)
    visible = (index[None, :] <= index[:, None]) & (doc_ids[None, :] == doc_ids[:, None])
    per_group = HEADS // KV_HEADS
    grouped_q = jnp.transpose(queries.reshape(count, KV_HEADS, per_group, HEAD_DIM), (1, 0, 2, 3))
    grouped_k = jnp.transpose(keys, (1, 0, 2))
    grouped_v = jnp.transpose(values, (1, 0, 2))

    def one_group(operands):
        q_group, k_group, v_group = operands
        scores = jnp.einsum('qhd,kd->hqk', q_group.astype(jnp.float32), k_group.astype(jnp.float32)) / jnp.sqrt(jnp.float32(HEAD_DIM))
        scores = jnp.where(visible[None], scores, jnp.float32(-1e+30))
        top = lax.optimization_barrier(jnp.max(scores, axis=-1, keepdims=True))
        weights = jnp.exp(scores - top)
        probs = (weights / lax.optimization_barrier(jnp.sum(weights, axis=-1, keepdims=True))).astype(jnp.bfloat16)
        return jnp.einsum('hqk,kd->qhd', probs.astype(jnp.float32), v_group.astype(jnp.float32)).astype(jnp.bfloat16)
    outs = lax.map(one_group, (grouped_q, grouped_k, grouped_v))
    attended = jnp.transpose(outs, (1, 0, 2, 3)).reshape(count, HEADS * HEAD_DIM)
    width = HEADS // N_TENSOR * HEAD_DIM

    def add_shard(total, shard):
        start = (shard * width).astype(jnp.int32)
        cols = lax.dynamic_slice_in_dim(attended, start, width, 1)
        weight_rows = lax.dynamic_slice_in_dim(w_output, start, width, 0)
        partial_value = jnp.dot(cols, weight_rows, preferred_element_type=jnp.float32).astype(jnp.bfloat16)
        return (total + partial_value.astype(jnp.float32), None)
    total, unused = lax.scan(add_shard, jnp.zeros((count, D), jnp.float32), jnp.arange(N_TENSOR, dtype=jnp.int32))
    return (total.astype(jnp.bfloat16), (rows + total).astype(jnp.bfloat16))
```

```python
import functools
import jax
import jax.numpy as jnp
from jax import lax
from jax.experimental import pallas as pl
from jax.experimental.pallas import tpu as pltpu
from jax.sharding import PartitionSpec as P

HEAD_DIM = 128
HALVES = 2
PARTS = 4
MESH = pl.DeviceIdType.MESH
F32 = jnp.float32
BF16 = jnp.bfloat16


def swapped(value, axis, apart):
    mask = 2**apart
    pairs = [(source, source ^ mask) for source in range(lax.axis_size(axis))]
    return lax.ppermute(value, axis, pairs)


def join_cols(mine, other, place, bit):
    upper = place // (1 << bit) % 2 == 1
    lower_part = jnp.where(upper, other, mine)
    upper_part = jnp.where(upper, mine, other)
    return jnp.concatenate([lower_part, upper_part], axis=-1)


def chip_of(n, pos):
    if n == 8:
        second = lax.div(pos, 4)
        level = pos + second * (7 - 2 * pos)
        return 2 * level + second
    return pos


def pos_of(n, chip):
    if n == 8:
        level, second = lax.div(chip, 2), lax.rem(chip, 2)
        return level + second * (7 - 2 * level)
    return chip


def kernel(
    n, heads, shared,
    tokens, gain, wq, wk, wv, wo, docs, freq,
    att_out, hid_out,
    normed, wq_v, raw, wkv_v, wo_v, q_v, k_v, v_v, att_v, att_in, cos_v, sin_v, doc_v, inbox,
    ring_s, ring_r, fwd_s, fwd_r, kv_s, kv_r, wo_s, wo_r, at_s, at_r, rs_s, rs_r, loc,
):
    rows, width = tokens.shape
    count = normed.shape[0]
    piece = rows // HALVES
    cols = width // PARTS
    place = lax.axis_index("tensor")
    core = lax.rem(place, 2)
    chip = lax.div(place, 2)
    pos = pos_of(n, chip)
    way = 1 - 2 * core
    other = {"tensor": 2 * chip + 1 - core}

    def at_pos(p):
        return lax.rem(p + 2 * n, n)

    nxt = {"tensor": 2 * chip_of(n, at_pos(pos + way)) + core}
    prv = {"tensor": 2 * chip_of(n, at_pos(pos - way)) + core}

    def block_row(p, c):
        return pl.multiple_of((2 * chip_of(n, at_pos(p)) + c) * rows, rows)

    def remote(src, dst, s_sem, r_sem, to):
        return pltpu.make_async_remote_copy(
            src_ref=src, dst_ref=dst, send_sem=s_sem, recv_sem=r_sem,
            device_id=to, device_id_type=MESH,
        )

    def piece_at(p, c, h):
        return normed.at[pl.ds(pl.multiple_of(block_row(p, c) + h * piece, piece), piece), :]

    def ring(s, h):
        ref = piece_at(pos - way * s, core, h)
        return remote(ref, ref, ring_s.at[s, h], ring_r.at[s, h], nxt)

    def ring_in(s, h):
        ref = piece_at(pos - way * (s + 1), core, h)
        return remote(ref, ref, ring_s.at[s, h], ring_r.at[s, h], nxt)

    def fwd(s, h):
        ref = piece_at(pos - way * s, core, h)
        return remote(ref, ref, fwd_s.at[s, h], fwd_r.at[s, h], other)

    def fwd_in(s, h):
        ref = piece_at(pos + way * s, 1 - core, h)
        return remote(ref, ref, fwd_s.at[s, h], fwd_r.at[s, h], other)

    wo_piece = wo.shape[0] // n

    def wo_copy(s, c):
        part = pl.ds(pl.multiple_of(s * wo_piece, wo_piece), wo_piece)
        return remote(wo.at[part, :], wo_v.at[c, part, :], wo_s.at[s], wo_r.at[s], other)

    local = [pltpu.make_async_copy(wq, wq_v, loc.at[0])]
    if shared:
        local += [
            pltpu.make_async_copy(wk, raw.at[core, 0], loc.at[1]),
            pltpu.make_async_copy(wv, raw.at[core, 1], loc.at[2]),
        ]
    else:
        local += [
            pltpu.make_async_copy(wk, wkv_v.at[:, 0:HEAD_DIM], loc.at[1]),
            pltpu.make_async_copy(wv, wkv_v.at[:, HEAD_DIM:], loc.at[2]),
        ]
    own_wo = pltpu.make_async_copy(wo, wo_v.at[core], loc.at[3])

    barrier = pltpu.get_barrier_semaphore()
    for to in (prv, other):
        pl.semaphore_signal(barrier, inc=1, device_id=to, device_id_type=MESH)

    x = tokens[...].astype(F32)
    scale = lax.rsqrt(jnp.mean(x * x, axis=-1, keepdims=True) + 1e-05)
    normed[pl.ds(block_row(pos, core), rows), :] = (x * scale * gain[...]).astype(BF16)

    pl.semaphore_wait(barrier, 2)
    for h in range(HALVES):
        ring(0, h).start()
    for h in range(HALVES):
        fwd(0, h).start()
    if shared:
        kv = [
            remote(wk, raw.at[core, 0], kv_s.at[0], kv_r.at[0], other),
            remote(wv, raw.at[core, 1], kv_s.at[1], kv_r.at[1], other),
        ]
        for c in kv:
            c.start()
    for c in local:
        c.start()
    own_wo.start()

    def tables():
        drow = docs[...].astype(F32)
        doc_v[...] = jnp.transpose(jnp.broadcast_to(drow, (HEAD_DIM, count)))
        lane = lax.broadcasted_iota(jnp.int32, (1, HEAD_DIM), 1)
        sign = jnp.where(lane < HEAD_DIM // 2, F32(-1.0), F32(1.0))
        tile = 128

        def one(i, carry):
            at = pl.ds(pl.multiple_of(i * tile, tile), tile)
            less = (drow < doc_v[at, 0:1]).astype(F32)
            first = jnp.sum(less, axis=1, keepdims=True)
            index = (lax.broadcasted_iota(jnp.int32, (tile, 1), 0) + i * tile).astype(F32)
            angle = (index - first) * freq[...]
            cos_v[at, :] = jnp.cos(angle)
            sin_v[at, :] = jnp.sin(angle) * sign
            return carry

        lax.fori_loop(0, count // tile, one, 0)

    def join():
        if not shared:
            return
        for i in range(2):
            remote(wk, raw.at[1 - core, i], kv_s.at[i], kv_r.at[i], other).wait_recv()
        tall = 512

        def one(i, carry):
            at = pl.ds(pl.multiple_of(i * tall, tall), tall)
            wkv_v[at, :] = jnp.concatenate(
                [raw[0, 0, at, :], raw[1, 0, at, :], raw[0, 1, at, :], raw[1, 1, at, :]], axis=1
            )
            return carry

        lax.fori_loop(0, width // tall, one, 0)

    def rope(u, at):
        return u * cos_v[at, :] + pltpu.roll(u, HEAD_DIM // 2, 1) * sin_v[at, :]

    deep = 1024

    def product(starts, weights):
        def one(i, acc):
            k = pl.ds(pl.multiple_of(i * deep, deep), deep)
            left = jnp.concatenate([normed[pl.ds(a, rows), k] for a in starts], axis=0)
            return acc + jnp.dot(left, weights[k, :], preferred_element_type=F32)

        start = jnp.zeros((rows * len(starts), weights.shape[1]), F32)
        return lax.fori_loop(0, width // deep, one, start)

    def do_queries(starts):
        raw_q = product(starts, wq_v)
        for i, a in enumerate(starts):
            at = pl.ds(a, rows)
            for h in range(heads):
                u = raw_q[i * rows : (i + 1) * rows, h * HEAD_DIM : (h + 1) * HEAD_DIM]
                q_v[at, h * HEAD_DIM : (h + 1) * HEAD_DIM] = rope(u, at).astype(BF16)

    def do_keys(starts):
        both = product(starts, wkv_v)
        for i, a in enumerate(starts):
            at = pl.ds(a, rows)
            u = both[i * rows : (i + 1) * rows, :].astype(BF16)
            k_v[at, :] = rope(u[:, :HEAD_DIM].astype(F32), at).astype(BF16)
            v_v[at, :] = u[:, HEAD_DIM:]

    def group(s):
        return [block_row(pos - way * s, core), block_row(pos + way * s, 1 - core)]

    def step(s, carry):
        wo_copy(s, core).start()
        for h in range(HALVES):
            ring_in(s, h).wait_recv()

            @pl.when(s < n - 2)
            def _():
                ring(s + 1, h).start()

            fwd(s + 1, h).start()
            if h == 0:

                @pl.when(s == 0)
                def _():
                    for c in local:
                        c.wait()
                    join()

                @pl.when(s > 0)
                def _():
                    for k in range(HALVES):
                        fwd_in(s - 1, k).wait_recv()
                    do_queries(group(s - 1))

            if h == HALVES - 1:

                @pl.when(s == 0)
                def _():
                    tables()

                @pl.when(s > 0)
                def _():
                    do_keys(group(s - 1))

        return carry

    lax.fori_loop(0, n - 1, step, 0)
    wo_copy(n - 1, core).start()
    for s in (n - 2, n - 1):
        for h in range(HALVES):
            fwd_in(s, h).wait_recv()
    last = group(n - 2) + group(n - 1)
    do_keys(last)
    do_queries(last)

    def sent(s, carry):
        for h in range(HALVES):
            fwd(s, h).wait_send()

            @pl.when(s < n - 1)
            def _():
                ring(s, h).wait_send()

        wo_copy(s, core).wait_send()
        return carry

    lax.fori_loop(0, n, sent, 0)
    if shared:
        for c in kv:
            c.wait_send()

    block = 128
    root = F32(1.0 / HEAD_DIM**0.5)
    for i in range(count // block):
        seen = (i + 1) * block
        span = slice(i * block, seen)
        r_idx = lax.broadcasted_iota(jnp.int32, (block, seen), 0) + i * block
        c_idx = lax.broadcasted_iota(jnp.int32, (block, seen), 1)
        visible = (c_idx <= r_idx) & (docs[:, :seen].astype(F32) == doc_v[span, 0:1])
        for h in range(heads):
            hs = slice(h * HEAD_DIM, (h + 1) * HEAD_DIM)
            scores = lax.dot_general(
                q_v[span, hs], k_v[0:seen, :], (((1,), (1,)), ((), ())),
                preferred_element_type=F32,
            )
            scores = jnp.where(visible, scores * root, F32(-1e30))
            weights = jnp.exp(scores - jnp.max(scores, axis=-1, keepdims=True))
            total = jnp.sum(weights, axis=-1, keepdims=True)
            probs = (weights * (1.0 / total)).astype(BF16)
            result = jnp.dot(probs, v_v[0:seen, :], preferred_element_type=F32).astype(BF16)
            for j in range(block // rows):
                t = i * (block // rows) + j
                att_v[t % 2, (t // 2) * rows : (t // 2 + 1) * rows, hs] = result[
                    j * rows : (j + 1) * rows
                ]

    swap = remote(att_v.at[1 - core], att_in, at_s.at[0], at_r.at[0], other)
    swap.start()
    own_wo.wait()

    def arrived(s, carry):
        wo_copy(s, 1 - core).wait_recv()
        return carry

    lax.fori_loop(0, n, arrived, 0)
    swap.wait()

    def part_row(p):
        return pl.multiple_of(chip_of(n, at_pos(p)) * rows, rows)

    def part_of(p, k):
        return (pl.ds(part_row(p), rows), slice(k * cols, (k + 1) * cols))

    def reduced(s, k, src):
        dst = inbox.at[s, :, k * cols : (k + 1) * cols]
        return remote(src, dst, rs_s.at[s, k], rs_r.at[s, k], nxt)

    def first_out(k):
        at, cs = part_of(pos - way, k)
        return reduced(0, k, normed.at[at, cs])

    def later_out(s, k):
        return reduced(s, k, inbox.at[s - 1, :, k * cols : (k + 1) * cols])

    thin = 256
    for k in range(PARTS):

        def one(i, carry):
            cs = pl.ds(pl.multiple_of(k * cols + i * thin, thin), thin)
            out = jnp.dot(att_v[core], wo_v[core, :, cs], preferred_element_type=F32)
            out += jnp.dot(att_in[...], wo_v[1 - core, :, cs], preferred_element_type=F32)
            normed[0 : n * rows, cs] = out.astype(BF16)
            return carry

        lax.fori_loop(0, cols // thin, one, 0)
        first_out(k).start()

    def hop(s, carry):
        for k in range(PARTS):
            cs = slice(k * cols, (k + 1) * cols)
            reduced(s - 1, k, inbox.at[s - 1, :, cs]).wait_recv()
            at, _ = part_of(pos - way * (s + 1), k)
            both = inbox[s - 1, :, cs].astype(F32) + normed[at, cs].astype(F32)
            inbox[s - 1, :, cs] = both.astype(BF16)
            later_out(s, k).start()
        return carry

    lax.fori_loop(1, n - 1, hop, 0)
    for k in range(PARTS):
        cs = slice(k * cols, (k + 1) * cols)
        reduced(n - 2, k, inbox.at[n - 2, :, cs]).wait_recv()
        at, _ = part_of(pos, k)
        total = inbox[n - 2, :, cs].astype(F32) + normed[at, cs].astype(F32)
        att_out[:, cs] = total.astype(BF16)
        hid_out[:, cs] = (tokens[:, cs].astype(F32) + total).astype(BF16)

    for k in range(PARTS):
        first_out(k).wait_send()

    def left(s, carry):
        for k in range(PARTS):
            later_out(s, k).wait_send()
        return carry

    lax.fori_loop(1, n - 1, left, 0)


def body(tokens, attn_gain, w_query, w_key, w_value, w_output, doc_ids):
    n = lax.axis_size("tensor") // 2
    rows, width = tokens.shape
    count = doc_ids.shape[0]
    mine = w_query.shape[1]
    heads = mine // HEAD_DIM
    levels = (HEAD_DIM // w_key.shape[1]).bit_length() - 1
    shared = levels == 1
    if not shared:
        place = lax.axis_index("tensor")
        stacked = jnp.stack([w_key, w_value])
        for bit in range(levels):
            stacked = join_cols(stacked, swapped(stacked, "tensor", bit), place, bit)
        w_key, w_value = stacked[0], stacked[1]
    freq = F32(500000.0) ** (
        -(jnp.arange(HEAD_DIM // 2, dtype=F32) * 2.0 / HEAD_DIM)
    )
    freq = jnp.concatenate([freq, freq])[None, :]
    vmem = pl.BlockSpec(memory_space=pltpu.VMEM)
    hbm = pl.BlockSpec(memory_space=pl.ANY)
    raw = (2, 2, width, w_key.shape[1]) if shared else (2, 2, 16, HEAD_DIM)
    dma = pltpu.SemaphoreType.DMA
    return pl.pallas_call(
        functools.partial(kernel, n, heads, shared),
        out_shape=(jax.ShapeDtypeStruct((rows, width), BF16),) * 2,
        in_specs=[vmem, vmem, hbm, hbm, hbm, hbm, vmem, vmem],
        out_specs=(vmem, vmem),
        scratch_shapes=[
            pltpu.VMEM((count, width), BF16),
            pltpu.VMEM((width, mine), BF16),
            pltpu.VMEM(raw, BF16),
            pltpu.VMEM((width, 2 * HEAD_DIM), BF16),
            pltpu.VMEM((2, mine, width), BF16),
            pltpu.VMEM((count, mine), BF16),
            pltpu.VMEM((count, HEAD_DIM), BF16),
            pltpu.VMEM((count, HEAD_DIM), BF16),
            pltpu.VMEM((2, n * rows, mine), BF16),
            pltpu.VMEM((n * rows, mine), BF16),
            pltpu.VMEM((count, HEAD_DIM), F32),
            pltpu.VMEM((count, HEAD_DIM), F32),
            pltpu.VMEM((count, HEAD_DIM), F32),
            pltpu.VMEM((n - 1, rows, width), BF16),
            dma((n - 1, HALVES)), dma((n - 1, HALVES)),
            dma((n, HALVES)), dma((n, HALVES)),
            dma((2,)), dma((2,)),
            dma((n,)), dma((n,)),
            dma((1,)), dma((1,)),
            dma((n - 1, PARTS)), dma((n - 1, PARTS)),
            dma((4,)),
        ],
        compiler_params=pltpu.CompilerParams(
            collective_id=0, has_side_effects=True, vmem_limit_bytes=60 * 1024 * 1024
        ),
    )(tokens, attn_gain[None, :], w_query, w_key, w_value, w_output, doc_ids[None, :], freq)


def solution(mesh):
    placed = (
        P(("groups", "tensor"), None),
        P(),
        P(None, "tensor"),
        P(None, "tensor"),
        P(None, "tensor"),
        P("tensor", None),
        P("groups"),
    )
    return jax.shard_map(
        body,
        mesh=mesh,
        in_specs=placed,
        out_specs=(P(("groups", "tensor"), None), P(("groups", "tensor"), None)),
        check_vma=False,
    )
```

```python
import functools
import jax
import jax.numpy as jnp
from jax import lax
from jax.experimental import pallas as pl
from jax.experimental.pallas import tpu as pltpu
from jax.sharding import PartitionSpec as P

HEAD_DIM = 128
HALVES = 2
PARTS = 4
MESH = pl.DeviceIdType.MESH
F32 = jnp.float32
BF16 = jnp.bfloat16


def swapped(value, axis, apart):
    mask = 2**apart
    pairs = [(source, source ^ mask) for source in range(lax.axis_size(axis))]
    return lax.ppermute(value, axis, pairs)


def join_cols(mine, other, place, bit):
    upper = place // (1 << bit) % 2 == 1
    lower_part = jnp.where(upper, other, mine)
    upper_part = jnp.where(upper, mine, other)
    return jnp.concatenate([lower_part, upper_part], axis=-1)


def chip_of(n, pos):
    if n == 8:
        second = lax.div(pos, 4)
        level = pos + second * (7 - 2 * pos)
        return 2 * level + second
    return pos


def pos_of(n, chip):
    if n == 8:
        level, second = lax.div(chip, 2), lax.rem(chip, 2)
        return level + second * (7 - 2 * level)
    return chip


def kernel(
    n, heads, shared,
    tokens, gain, wq, wk, wv, wo, docs, freq,
    total_out,
    normed, wq_v, wkv_v, wo_v, q_v, k_v, v_v, att_v, att_in, cos_v, sin_v, doc_v, inbox,
    ring_s, ring_r, fwd_s, fwd_r, kv_s, kv_r, wo_s, wo_r, at_s, at_r, rs_s, rs_r, loc,
):
    rows, width = tokens.shape
    count = normed.shape[0]
    piece = rows // HALVES
    cols = width // PARTS
    place = lax.axis_index("tensor")
    core = lax.rem(place, 2)
    chip = lax.div(place, 2)
    pos = pos_of(n, chip)
    way = 1 - 2 * core
    other = {"tensor": 2 * chip + 1 - core}

    def at_pos(p):
        return lax.rem(p + 2 * n, n)

    nxt = {"tensor": 2 * chip_of(n, at_pos(pos + way)) + core}
    prv = {"tensor": 2 * chip_of(n, at_pos(pos - way)) + core}

    def block_row(p, c):
        return pl.multiple_of((2 * chip_of(n, at_pos(p)) + c) * rows, rows)

    def remote(src, dst, s_sem, r_sem, to):
        return pltpu.make_async_remote_copy(
            src_ref=src, dst_ref=dst, send_sem=s_sem, recv_sem=r_sem,
            device_id=to, device_id_type=MESH,
        )

    def piece_at(p, c, h):
        return normed.at[pl.ds(pl.multiple_of(block_row(p, c) + h * piece, piece), piece), :]

    def ring(s, h):
        ref = piece_at(pos - way * s, core, h)
        return remote(ref, ref, ring_s.at[s, h], ring_r.at[s, h], nxt)

    def ring_in(s, h):
        ref = piece_at(pos - way * (s + 1), core, h)
        return remote(ref, ref, ring_s.at[s, h], ring_r.at[s, h], nxt)

    def fwd(s, h):
        ref = piece_at(pos - way * s, core, h)
        return remote(ref, ref, fwd_s.at[s, h], fwd_r.at[s, h], other)

    def fwd_in(s, h):
        ref = piece_at(pos + way * s, 1 - core, h)
        return remote(ref, ref, fwd_s.at[s, h], fwd_r.at[s, h], other)

    wo_piece = wo.shape[0] // n

    def wo_copy(s, c):
        part = pl.ds(pl.multiple_of(s * wo_piece, wo_piece), wo_piece)
        return remote(wo.at[part, :], wo_v.at[c, part, :], wo_s.at[s], wo_r.at[s], other)

    kv_rows = wk.shape[0]

    def kv_slot(c, i):
        start = i * HEAD_DIM + (c * kv_rows if shared else 0)
        return wkv_v.at[pl.ds(pl.multiple_of(start, 16), kv_rows), :]

    local = [
        pltpu.make_async_copy(wk, kv_slot(core, 0), loc.at[1]),
        pltpu.make_async_copy(wv, kv_slot(core, 1), loc.at[2]),
        pltpu.make_async_copy(wq, wq_v, loc.at[0]),
    ]
    own_wo = pltpu.make_async_copy(wo, wo_v.at[core], loc.at[3])

    barrier = pltpu.get_barrier_semaphore()
    for to in (prv, other):
        pl.semaphore_signal(barrier, inc=1, device_id=to, device_id_type=MESH)

    x = tokens[...].astype(F32)
    scale = lax.rsqrt(jnp.mean(x * x, axis=-1, keepdims=True) + 1e-05)
    normed[pl.ds(block_row(pos, core), rows), :] = (x * scale * gain[...]).astype(BF16)

    pl.semaphore_wait(barrier, 2)
    for h in range(HALVES):
        ring(0, h).start()
    for h in range(HALVES):
        fwd(0, h).start()
    if shared:
        kv = [
            remote(wk, kv_slot(core, 0), kv_s.at[0], kv_r.at[0], other),
            remote(wv, kv_slot(core, 1), kv_s.at[1], kv_r.at[1], other),
        ]
        for c in kv:
            c.start()
    for c in local:
        c.start()
    own_wo.start()

    def tables():
        drow = docs[...].astype(F32)
        doc_v[...] = jnp.transpose(jnp.broadcast_to(drow, (HEAD_DIM, count)))
        lane = lax.broadcasted_iota(jnp.int32, (1, HEAD_DIM), 1)
        sign = jnp.where(lane < HEAD_DIM // 2, F32(-1.0), F32(1.0))
        tile = 128

        def one(i, carry):
            at = pl.ds(pl.multiple_of(i * tile, tile), tile)
            less = (drow < doc_v[at, 0:1]).astype(F32)
            first = jnp.sum(less, axis=1, keepdims=True)
            index = (lax.broadcasted_iota(jnp.int32, (tile, 1), 0) + i * tile).astype(F32)
            angle = (index - first) * freq[...]
            cos_v[at, :] = jnp.cos(angle)
            sin_v[at, :] = jnp.sin(angle) * sign
            return carry

        lax.fori_loop(0, count // tile, one, 0)

    def weights_in():
        for c in local:
            c.wait()
        if shared:
            for i in range(2):
                remote(wk, kv_slot(1 - core, i), kv_s.at[i], kv_r.at[i], other).wait_recv()

    def rope(u, at):
        return u * cos_v[at, :] + pltpu.roll(u, HEAD_DIM // 2, 1) * sin_v[at, :]

    deep = 1024

    def product(starts, weights, turned):
        size = weights.shape[0] if turned else weights.shape[1]

        def one(i, acc):
            k = pl.ds(pl.multiple_of(i * deep, deep), deep)
            left = jnp.concatenate([normed[pl.ds(a, rows), k] for a in starts], axis=0)
            if turned:
                return acc + lax.dot_general(
                    left, weights[:, k], (((1,), (1,)), ((), ())), preferred_element_type=F32
                )
            return acc + jnp.dot(left, weights[k, :], preferred_element_type=F32)

        start = jnp.zeros((rows * len(starts), size), F32)
        return lax.fori_loop(0, width // deep, one, start)

    def do_queries(starts):
        raw_q = product(starts, wq_v, False)
        for i, a in enumerate(starts):
            at = pl.ds(a, rows)
            for h in range(heads):
                u = raw_q[i * rows : (i + 1) * rows, h * HEAD_DIM : (h + 1) * HEAD_DIM]
                q_v[at, h * HEAD_DIM : (h + 1) * HEAD_DIM] = rope(u, at).astype(BF16)

    def do_keys(starts):
        both = product(starts, wkv_v, True)
        for i, a in enumerate(starts):
            at = pl.ds(a, rows)
            u = both[i * rows : (i + 1) * rows, :].astype(BF16)
            k_v[at, :] = rope(u[:, :HEAD_DIM].astype(F32), at).astype(BF16)
            v_v[at, :] = u[:, HEAD_DIM:]

    def group(s):
        return [block_row(pos - way * s, core), block_row(pos + way * s, 1 - core)]

    def step(s, carry):
        wo_copy(s, core).start()
        for h in range(HALVES):
            ring_in(s, h).wait_recv()

            @pl.when(s < n - 2)
            def _():
                ring(s + 1, h).start()

            fwd(s + 1, h).start()
            if h == 0:

                @pl.when(s == 0)
                def _():
                    tables()

                @pl.when(s == 1)
                def _():
                    weights_in()
                    for t in range(2):
                        for k in range(HALVES):
                            fwd_in(t, k).wait_recv()
                    do_queries(group(0) + group(1))

                @pl.when(s > 1)
                def _():
                    for k in range(HALVES):
                        fwd_in(s, k).wait_recv()
                    do_queries(group(s))

            if h == HALVES - 1:

                @pl.when(s == 1)
                def _():
                    do_keys(group(0) + group(1))

                @pl.when(s > 1)
                def _():
                    do_keys(group(s))

        return carry

    lax.fori_loop(0, n - 1, step, 0)
    wo_copy(n - 1, core).start()
    for h in range(HALVES):
        fwd_in(n - 1, h).wait_recv()
    do_keys(group(n - 1))
    do_queries(group(n - 1))

    def sent(s, carry):
        for h in range(HALVES):
            fwd(s, h).wait_send()

            @pl.when(s < n - 1)
            def _():
                ring(s, h).wait_send()

        wo_copy(s, core).wait_send()
        return carry

    lax.fori_loop(0, n, sent, 0)
    if shared:
        for c in kv:
            c.wait_send()

    block = 128
    root = F32(1.0 / HEAD_DIM**0.5)
    swaps = []
    for i in reversed(range(count // block)):
        seen = (i + 1) * block
        span = slice(i * block, seen)
        r_idx = lax.broadcasted_iota(jnp.int32, (block, seen), 0) + i * block
        c_idx = lax.broadcasted_iota(jnp.int32, (block, seen), 1)
        visible = (c_idx <= r_idx) & (docs[:, :seen].astype(F32) == doc_v[span, 0:1])
        for h in range(heads):
            hs = slice(h * HEAD_DIM, (h + 1) * HEAD_DIM)
            scores = lax.dot_general(
                q_v[span, hs], k_v[0:seen, :], (((1,), (1,)), ((), ())),
                preferred_element_type=F32,
            )
            scores = jnp.where(visible, scores * root, F32(-1e30))
            weights = jnp.exp(scores - jnp.max(scores, axis=-1, keepdims=True))
            total = jnp.sum(weights, axis=-1, keepdims=True)
            probs = (weights * (1.0 / total)).astype(BF16)
            result = jnp.dot(probs, v_v[0:seen, :], preferred_element_type=F32).astype(BF16)
            for j in range(block // rows):
                t = i * (block // rows) + j
                att_v[t % 2, (t // 2) * rows : (t // 2 + 1) * rows, hs] = result[
                    j * rows : (j + 1) * rows
                ]

        part = pl.ds(i * block // 2, block // 2)
        swap = remote(
            att_v.at[1 - core, part, :], att_in.at[part, :], at_s.at[i], at_r.at[i], other
        )
        swap.start()
        swaps.append(swap)
    own_wo.wait()

    def arrived(s, carry):
        wo_copy(s, 1 - core).wait_recv()
        return carry

    lax.fori_loop(0, n, arrived, 0)
    for swap in swaps:
        swap.wait()

    def part_row(p):
        return pl.multiple_of(chip_of(n, at_pos(p)) * rows, rows)

    def part_of(p, k):
        return (pl.ds(part_row(p), rows), slice(k * cols, (k + 1) * cols))

    def reduced(s, k, src):
        dst = inbox.at[s, :, k * cols : (k + 1) * cols]
        return remote(src, dst, rs_s.at[s, k], rs_r.at[s, k], nxt)

    def first_out(k):
        at, cs = part_of(pos - way, k)
        return reduced(0, k, normed.at[at, cs])

    def later_out(s, k):
        return reduced(s, k, inbox.at[s - 1, :, k * cols : (k + 1) * cols])

    thin = 256
    for k in range(PARTS):

        def one(i, carry):
            cs = pl.ds(pl.multiple_of(k * cols + i * thin, thin), thin)
            out = jnp.dot(att_v[core], wo_v[core, :, cs], preferred_element_type=F32)
            out += jnp.dot(att_in[...], wo_v[1 - core, :, cs], preferred_element_type=F32)
            normed[0 : n * rows, cs] = out.astype(BF16)
            return carry

        lax.fori_loop(0, cols // thin, one, 0)
        first_out(k).start()

    def hop(s, carry):
        for k in range(PARTS):
            cs = slice(k * cols, (k + 1) * cols)
            reduced(s - 1, k, inbox.at[s - 1, :, cs]).wait_recv()
            at, _ = part_of(pos - way * (s + 1), k)
            both = inbox[s - 1, :, cs].astype(F32) + normed[at, cs].astype(F32)
            inbox[s - 1, :, cs] = both.astype(BF16)
            later_out(s, k).start()
        return carry

    lax.fori_loop(1, n - 1, hop, 0)
    for k in range(PARTS):
        cs = slice(k * cols, (k + 1) * cols)
        reduced(n - 2, k, inbox.at[n - 2, :, cs]).wait_recv()
        at, _ = part_of(pos, k)
        total = inbox[n - 2, :, cs].astype(F32) + normed[at, cs].astype(F32)
        total_out[:, cs] = total

    for k in range(PARTS):
        first_out(k).wait_send()

    def left(s, carry):
        for k in range(PARTS):
            later_out(s, k).wait_send()
        return carry

    lax.fori_loop(1, n - 1, left, 0)


def body(tokens, attn_gain, w_query, w_key, w_value, w_output, doc_ids):
    n = lax.axis_size("tensor") // 2
    rows, width = tokens.shape
    count = doc_ids.shape[0]
    mine = w_query.shape[1]
    heads = mine // HEAD_DIM
    levels = (HEAD_DIM // w_key.shape[1]).bit_length() - 1
    shared = levels == 1
    if not shared:
        place = lax.axis_index("tensor")
        stacked = jnp.stack([w_key, w_value])
        for bit in range(levels):
            stacked = join_cols(stacked, swapped(stacked, "tensor", bit), place, bit)
        w_key, w_value = stacked[0], stacked[1]
    freq = F32(500000.0) ** (
        -(jnp.arange(HEAD_DIM // 2, dtype=F32) * 2.0 / HEAD_DIM)
    )
    freq = jnp.concatenate([freq, freq])[None, :]
    vmem = pl.BlockSpec(memory_space=pltpu.VMEM)
    hbm = pl.BlockSpec(memory_space=pl.ANY)
    dma = pltpu.SemaphoreType.DMA
    total = pl.pallas_call(
        functools.partial(kernel, n, heads, shared),
        out_shape=jax.ShapeDtypeStruct((rows, width), F32),
        in_specs=[vmem, vmem, hbm, hbm, hbm, hbm, vmem, vmem],
        out_specs=vmem,
        scratch_shapes=[
            pltpu.VMEM((count, width), BF16),
            pltpu.VMEM((width, mine), BF16),
            pltpu.VMEM((2 * HEAD_DIM, width), BF16),
            pltpu.VMEM((2, mine, width), BF16),
            pltpu.VMEM((count, mine), BF16),
            pltpu.VMEM((count, HEAD_DIM), BF16),
            pltpu.VMEM((count, HEAD_DIM), BF16),
            pltpu.VMEM((2, n * rows, mine), BF16),
            pltpu.VMEM((n * rows, mine), BF16),
            pltpu.VMEM((count, HEAD_DIM), F32),
            pltpu.VMEM((count, HEAD_DIM), F32),
            pltpu.VMEM((count, HEAD_DIM), F32),
            pltpu.VMEM((n - 1, rows, width), BF16),
            dma((n - 1, HALVES)), dma((n - 1, HALVES)),
            dma((n, HALVES)), dma((n, HALVES)),
            dma((2,)), dma((2,)),
            dma((n,)), dma((n,)),
            dma((count // 128,)), dma((count // 128,)),
            dma((n - 1, PARTS)), dma((n - 1, PARTS)),
            dma((4,)),
        ],
        compiler_params=pltpu.CompilerParams(
            collective_id=0, has_side_effects=True, vmem_limit_bytes=60 * 1024 * 1024
        ),
    )(tokens, attn_gain[None, :], w_query, w_key.T, w_value.T, w_output, doc_ids[None, :], freq)
    return (total.astype(BF16), (tokens.astype(F32) + total).astype(BF16))


def solution(mesh):
    placed = (
        P(("groups", "tensor"), None),
        P(),
        P(None, "tensor"),
        P(None, "tensor"),
        P(None, "tensor"),
        P("tensor", None),
        P("groups"),
    )
    return jax.shard_map(
        body,
        mesh=mesh,
        in_specs=placed,
        out_specs=(P(("groups", "tensor"), None), P(("groups", "tensor"), None)),
        check_vma=False,
    )
```

```python
import functools
import math
import jax
import jax.numpy as jnp
from jax import lax
from jax.experimental import pallas as pl
from jax.experimental.pallas import tpu as pltpu
from jax.sharding import PartitionSpec as P

HEAD_DIM = 128
HALVES = 2
PARTS = 8
MESH = pl.DeviceIdType.MESH
F32 = jnp.float32
BF16 = jnp.bfloat16


def swapped(value, axis, apart):
    mask = 2**apart
    pairs = [(source, source ^ mask) for source in range(lax.axis_size(axis))]
    return lax.ppermute(value, axis, pairs)


def join_cols(mine, other, place, bit):
    upper = place // (1 << bit) % 2 == 1
    lower_part = jnp.where(upper, other, mine)
    upper_part = jnp.where(upper, mine, other)
    return jnp.concatenate([lower_part, upper_part], axis=-1)


def chip_of(n, pos):
    if n == 8:
        second = lax.div(pos, 4)
        level = pos + second * (7 - 2 * pos)
        return 2 * level + second
    return pos


def pos_of(n, chip):
    if n == 8:
        level, second = lax.div(chip, 2), lax.rem(chip, 2)
        return level + second * (7 - 2 * level)
    return chip


def kernel(
    n, heads, shared,
    tokens, gain, wq, wk, wv, wo, docs,
    total_out,
    normed, wq_v, wkv_v, wo_v, q_v, k_v, v_v, att_v, att_in, cos_v, sin_v, doc_v, inbox,
    ring_s, ring_r, fwd_s, fwd_r, kv_s, kv_r, wo_s, wo_r, at_s, at_r, rs_s, rs_r, loc,
):
    rows, width = tokens.shape
    count = normed.shape[0]
    piece = rows // HALVES
    cols = width // PARTS
    place = lax.axis_index("tensor")
    core = lax.rem(place, 2)
    chip = lax.div(place, 2)
    pos = pos_of(n, chip)
    way = 1 - 2 * core
    other = {"tensor": 2 * chip + 1 - core}

    def at_pos(p):
        return lax.rem(p + 2 * n, n)

    nxt = {"tensor": 2 * chip_of(n, at_pos(pos + way)) + core}
    prv = {"tensor": 2 * chip_of(n, at_pos(pos - way)) + core}

    def block_row(p, c):
        return pl.multiple_of((2 * chip_of(n, at_pos(p)) + c) * rows, rows)

    def remote(src, dst, s_sem, r_sem, to):
        return pltpu.make_async_remote_copy(
            src_ref=src, dst_ref=dst, send_sem=s_sem, recv_sem=r_sem,
            device_id=to, device_id_type=MESH,
        )

    def piece_at(p, c, h):
        return normed.at[pl.ds(pl.multiple_of(block_row(p, c) + h * piece, piece), piece), :]

    def ring(s, h):
        ref = piece_at(pos - way * s, core, h)
        return remote(ref, ref, ring_s.at[s, h], ring_r.at[s, h], nxt)

    def ring_in(s, h):
        ref = piece_at(pos - way * (s + 1), core, h)
        return remote(ref, ref, ring_s.at[s, h], ring_r.at[s, h], nxt)

    def fwd(s, h):
        ref = piece_at(pos - way * s, core, h)
        return remote(ref, ref, fwd_s.at[s, h], fwd_r.at[s, h], other)

    def fwd_in(s, h):
        ref = piece_at(pos + way * s, 1 - core, h)
        return remote(ref, ref, fwd_s.at[s, h], fwd_r.at[s, h], other)

    wo_piece = wo.shape[0] // n

    def wo_copy(s, c):
        part = pl.ds(pl.multiple_of(s * wo_piece, wo_piece), wo_piece)
        return remote(wo.at[part, :], wo_v.at[c, part, :], wo_s.at[s], wo_r.at[s], other)

    kv_rows = wk.shape[0]

    def kv_slot(c, i):
        start = i * HEAD_DIM + (c * kv_rows if shared else 0)
        return wkv_v.at[pl.ds(pl.multiple_of(start, 16), kv_rows), :]

    local = [
        pltpu.make_async_copy(wk, kv_slot(core, 0), loc.at[1]),
        pltpu.make_async_copy(wv, kv_slot(core, 1), loc.at[2]),
        pltpu.make_async_copy(wq, wq_v, loc.at[0]),
    ]
    own_wo = pltpu.make_async_copy(wo, wo_v.at[core], loc.at[3])

    barrier = pltpu.get_barrier_semaphore()
    for to in (prv, other):
        pl.semaphore_signal(barrier, inc=1, device_id=to, device_id_type=MESH)

    for h in range(HALVES):
        x = tokens[h * piece : (h + 1) * piece, :].astype(F32)
        scale = lax.rsqrt(jnp.mean(x * x, axis=-1, keepdims=True) + 1e-05)
        at = pl.ds(pl.multiple_of(block_row(pos, core) + h * piece, piece), piece)
        normed[at, :] = (x * scale * gain[...]).astype(BF16)
        if h == 0:
            pl.semaphore_wait(barrier, 2)
        ring(0, h).start()
    for h in range(HALVES):
        fwd(0, h).start()
    if shared:
        kv = [
            remote(wk, kv_slot(core, 0), kv_s.at[0], kv_r.at[0], other),
            remote(wv, kv_slot(core, 1), kv_s.at[1], kv_r.at[1], other),
        ]
        for c in kv:
            c.start()
    for c in local:
        c.start()
    own_wo.start()

    def tables():
        drow = docs[...].astype(F32)
        doc_v[...] = jnp.transpose(jnp.broadcast_to(drow, (HEAD_DIM, count)))
        lane = lax.broadcasted_iota(jnp.int32, (1, HEAD_DIM), 1)
        sign = jnp.where(lane < HEAD_DIM // 2, F32(-1.0), F32(1.0))
        half = lax.rem(lane, HEAD_DIM // 2).astype(F32)
        freq = jnp.exp(half * F32(-2.0 * math.log(500000.0) / HEAD_DIM))
        tile = 128

        def one(i, carry):
            at = pl.ds(pl.multiple_of(i * tile, tile), tile)
            less = (drow < doc_v[at, 0:1]).astype(F32)
            first = jnp.sum(less, axis=1, keepdims=True)
            index = (lax.broadcasted_iota(jnp.int32, (tile, 1), 0) + i * tile).astype(F32)
            angle = (index - first) * freq
            cos_v[at, :] = jnp.cos(angle)
            sin_v[at, :] = jnp.sin(angle) * sign
            return carry

        lax.fori_loop(0, count // tile, one, 0)

    def weights_in():
        for c in local:
            c.wait()
        if shared:
            for i in range(2):
                remote(wk, kv_slot(1 - core, i), kv_s.at[i], kv_r.at[i], other).wait_recv()

    def rope(u, at):
        return u * cos_v[at, :] + pltpu.roll(u, HEAD_DIM // 2, 1) * sin_v[at, :]

    deep = 4096

    def product(starts, weights, turned):
        size = weights.shape[0] if turned else weights.shape[1]

        def one(i, acc):
            k = pl.ds(pl.multiple_of(i * deep, deep), deep)
            left = jnp.concatenate([normed[pl.ds(a, rows), k] for a in starts], axis=0)
            if turned:
                return acc + lax.dot_general(
                    left, weights[:, k], (((1,), (1,)), ((), ())), preferred_element_type=F32
                )
            return acc + jnp.dot(left, weights[k, :], preferred_element_type=F32)

        start = jnp.zeros((rows * len(starts), size), F32)
        return lax.fori_loop(0, width // deep, one, start)

    def do_queries(starts):
        raw_q = product(starts, wq_v, False)
        for i, a in enumerate(starts):
            at = pl.ds(a, rows)
            for h in range(heads):
                u = raw_q[i * rows : (i + 1) * rows, h * HEAD_DIM : (h + 1) * HEAD_DIM]
                q_v[at, h * HEAD_DIM : (h + 1) * HEAD_DIM] = rope(u, at).astype(BF16)

    def do_keys(starts):
        both = product(starts, wkv_v, True)
        for i, a in enumerate(starts):
            at = pl.ds(a, rows)
            u = both[i * rows : (i + 1) * rows, :].astype(BF16)
            k_v[at, :] = rope(u[:, :HEAD_DIM].astype(F32), at).astype(BF16)
            v_v[at, :] = u[:, HEAD_DIM:]

    def group(s):
        return [block_row(pos - way * s, core), block_row(pos + way * s, 1 - core)]

    def step(s, carry):
        wo_copy(s, core).start()
        for h in range(HALVES):
            ring_in(s, h).wait_recv()

            @pl.when(s < n - 2)
            def _():
                ring(s + 1, h).start()

            fwd(s + 1, h).start()
            if h == 0:

                @pl.when(s == 0)
                def _():
                    tables()

                @pl.when(s == 1)
                def _():
                    weights_in()
                    for t in range(2):
                        for k in range(HALVES):
                            fwd_in(t, k).wait_recv()
                    do_queries(group(0) + group(1))

                @pl.when(s > 1)
                def _():
                    for k in range(HALVES):
                        fwd_in(s, k).wait_recv()
                    do_queries(group(s))

            if h == HALVES - 1:

                @pl.when(s == 1)
                def _():
                    do_keys(group(0) + group(1))

                @pl.when(s > 1)
                def _():
                    do_keys(group(s))

        return carry

    lax.fori_loop(0, n - 1, step, 0)
    wo_copy(n - 1, core).start()
    for h in range(HALVES):
        fwd_in(n - 1, h).wait_recv()
    do_keys(group(n - 1))
    do_queries(group(n - 1))

    def sent(s, carry):
        for h in range(HALVES):
            fwd(s, h).wait_send()

            @pl.when(s < n - 1)
            def _():
                ring(s, h).wait_send()

        wo_copy(s, core).wait_send()
        return carry

    lax.fori_loop(0, n, sent, 0)
    if shared:
        for c in kv:
            c.wait_send()

    block = 128
    root = F32(1.0 / HEAD_DIM**0.5)
    swaps = []
    for i in reversed(range(count // block)):
        seen = (i + 1) * block
        span = slice(i * block, seen)
        r_idx = lax.broadcasted_iota(jnp.int32, (block, seen), 0) + i * block
        c_idx = lax.broadcasted_iota(jnp.int32, (block, seen), 1)
        visible = (c_idx <= r_idx) & (docs[:, :seen].astype(F32) == doc_v[span, 0:1])
        queries = jnp.concatenate(
            [q_v[span, h * HEAD_DIM : (h + 1) * HEAD_DIM] for h in range(heads)], axis=0
        )
        scores = lax.dot_general(
            queries, k_v[0:seen, :], (((1,), (1,)), ((), ())), preferred_element_type=F32
        ).reshape(heads, block, seen)
        scores = jnp.where(visible[None], scores * root, F32(-1e30))
        weights = jnp.exp(scores - jnp.max(scores, axis=-1, keepdims=True))
        total = jnp.sum(weights, axis=-1, keepdims=True)
        probs = (weights * (1.0 / total)).astype(BF16).reshape(heads * block, seen)
        result = jnp.dot(probs, v_v[0:seen, :], preferred_element_type=F32).astype(BF16)
        for h in range(heads):
            for j in range(block // rows):
                t = i * (block // rows) + j
                att_v[t % 2, (t // 2) * rows : (t // 2 + 1) * rows, h * HEAD_DIM : (h + 1) * HEAD_DIM] = result[
                    h * block + j * rows : h * block + (j + 1) * rows
                ]
        part = pl.ds(i * block // 2, block // 2)
        swap = remote(
            att_v.at[1 - core, part, :], att_in.at[part, :], at_s.at[i], at_r.at[i], other
        )
        swap.start()
        swaps.append(swap)
    own_wo.wait()

    def arrived(s, carry):
        wo_copy(s, 1 - core).wait_recv()
        return carry

    lax.fori_loop(0, n, arrived, 0)
    for swap in swaps:
        swap.wait()

    def part_row(p):
        return pl.multiple_of(chip_of(n, at_pos(p)) * rows, rows)

    def part_of(p, k):
        return (pl.ds(part_row(p), rows), slice(k * cols, (k + 1) * cols))

    def reduced(s, k, src):
        dst = inbox.at[s, :, k * cols : (k + 1) * cols]
        return remote(src, dst, rs_s.at[s, k], rs_r.at[s, k], nxt)

    def first_out(k):
        at, cs = part_of(pos - way, k)
        return reduced(0, k, normed.at[at, cs])

    def later_out(s, k):
        return reduced(s, k, inbox.at[s - 1, :, k * cols : (k + 1) * cols])

    thin = 1024
    for k in range(PARTS):

        def one(i, carry):
            cs = pl.ds(pl.multiple_of(k * cols + i * thin, thin), thin)
            left = jnp.concatenate([att_v[core], att_in[...]], axis=1)
            right = jnp.concatenate([wo_v[core, :, cs], wo_v[1 - core, :, cs]], axis=0)
            out = jnp.dot(left, right, preferred_element_type=F32)
            normed[0 : n * rows, cs] = out.astype(BF16)
            return carry

        lax.fori_loop(0, cols // thin, one, 0)
        first_out(k).start()

    def hop(s, carry):
        for k in range(PARTS):
            cs = slice(k * cols, (k + 1) * cols)
            reduced(s - 1, k, inbox.at[s - 1, :, cs]).wait_recv()
            at, _ = part_of(pos - way * (s + 1), k)
            both = inbox[s - 1, :, cs].astype(F32) + normed[at, cs].astype(F32)
            inbox[s - 1, :, cs] = both.astype(BF16)
            later_out(s, k).start()
        return carry

    lax.fori_loop(1, n - 1, hop, 0)
    for k in range(PARTS):
        cs = slice(k * cols, (k + 1) * cols)
        reduced(n - 2, k, inbox.at[n - 2, :, cs]).wait_recv()
        at, _ = part_of(pos, k)
        total = inbox[n - 2, :, cs].astype(F32) + normed[at, cs].astype(F32)
        total_out[:, cs] = total

    for k in range(PARTS):
        first_out(k).wait_send()

    def left(s, carry):
        for k in range(PARTS):
            later_out(s, k).wait_send()
        return carry

    lax.fori_loop(1, n - 1, left, 0)


def body(tokens, attn_gain, w_query, w_key, w_value, w_output, doc_ids):
    n = lax.axis_size("tensor") // 2
    rows, width = tokens.shape
    count = doc_ids.shape[0]
    mine = w_query.shape[1]
    heads = mine // HEAD_DIM
    levels = (HEAD_DIM // w_key.shape[1]).bit_length() - 1
    shared = levels == 1
    if not shared:
        place = lax.axis_index("tensor")
        stacked = jnp.stack([w_key, w_value])
        for bit in range(levels):
            stacked = join_cols(stacked, swapped(stacked, "tensor", bit), place, bit)
        w_key, w_value = stacked[0], stacked[1]
    vmem = pl.BlockSpec(memory_space=pltpu.VMEM)
    hbm = pl.BlockSpec(memory_space=pl.ANY)
    dma = pltpu.SemaphoreType.DMA
    total = pl.pallas_call(
        functools.partial(kernel, n, heads, shared),
        out_shape=jax.ShapeDtypeStruct((rows, width), F32),
        in_specs=[vmem, vmem, hbm, hbm, hbm, hbm, vmem],
        out_specs=vmem,
        scratch_shapes=[
            pltpu.VMEM((count, width), BF16),
            pltpu.VMEM((width, mine), BF16),
            pltpu.VMEM((2 * HEAD_DIM, width), BF16),
            pltpu.VMEM((2, mine, width), BF16),
            pltpu.VMEM((count, mine), BF16),
            pltpu.VMEM((count, HEAD_DIM), BF16),
            pltpu.VMEM((count, HEAD_DIM), BF16),
            pltpu.VMEM((2, n * rows, mine), BF16),
            pltpu.VMEM((n * rows, mine), BF16),
            pltpu.VMEM((count, HEAD_DIM), F32),
            pltpu.VMEM((count, HEAD_DIM), F32),
            pltpu.VMEM((count, HEAD_DIM), F32),
            pltpu.VMEM((n - 1, rows, width), BF16),
            dma((n - 1, HALVES)), dma((n - 1, HALVES)),
            dma((n, HALVES)), dma((n, HALVES)),
            dma((2,)), dma((2,)),
            dma((n,)), dma((n,)),
            dma((count // 128,)), dma((count // 128,)),
            dma((n - 1, PARTS)), dma((n - 1, PARTS)),
            dma((4,)),
        ],
        compiler_params=pltpu.CompilerParams(
            collective_id=0, has_side_effects=True, vmem_limit_bytes=60 * 1024 * 1024
        ),
    )(tokens, attn_gain[None, :], w_query, w_key.T, w_value.T, w_output, doc_ids[None, :])
    return (total.astype(BF16), (tokens.astype(F32) + total).astype(BF16))


def solution(mesh):
    placed = (
        P(("groups", "tensor"), None),
        P(),
        P(None, "tensor"),
        P(None, "tensor"),
        P(None, "tensor"),
        P("tensor", None),
        P("groups"),
    )
    return jax.shard_map(
        body,
        mesh=mesh,
        in_specs=placed,
        out_specs=(P(("groups", "tensor"), None), P(("groups", "tensor"), None)),
        check_vma=False,
    )
```

```python
import functools
import math
import jax
import jax.numpy as jnp
from jax import lax
from jax.experimental import pallas as pl
from jax.experimental.pallas import tpu as pltpu
from jax.sharding import PartitionSpec as P

HEAD_DIM = 128
HALVES = 2
PARTS = 8
MESH = pl.DeviceIdType.MESH
F32 = jnp.float32
BF16 = jnp.bfloat16


def swapped(value, axis, apart):
    mask = 2**apart
    pairs = [(source, source ^ mask) for source in range(lax.axis_size(axis))]
    return lax.ppermute(value, axis, pairs)


def join_cols(mine, other, place, bit):
    upper = place // (1 << bit) % 2 == 1
    lower_part = jnp.where(upper, other, mine)
    upper_part = jnp.where(upper, mine, other)
    return jnp.concatenate([lower_part, upper_part], axis=-1)


def chip_of(n, pos):
    if n == 8:
        second = lax.div(pos, 4)
        level = pos + second * (7 - 2 * pos)
        return 2 * level + second
    return pos


def pos_of(n, chip):
    if n == 8:
        level, second = lax.div(chip, 2), lax.rem(chip, 2)
        return level + second * (7 - 2 * level)
    return chip


def kernel(
    n, heads, shared,
    tokens, gain, wq, wk, wv, wo, docs,
    total_out,
    normed, wq_v, wkv_v, wo_v, q_v, k_v, v_v, att_v, att_in, cos_v, sin_v, doc_v, inbox,
    ring_s, ring_r, fwd_s, fwd_r, kv_s, kv_r, wo_s, wo_r, at_s, at_r, rs_s, rs_r, loc,
):
    rows, width = tokens.shape
    count = normed.shape[0]
    piece = rows // HALVES
    cols = width // PARTS
    place = lax.axis_index("tensor")
    core = lax.rem(place, 2)
    chip = lax.div(place, 2)
    pos = pos_of(n, chip)
    way = 1 - 2 * core
    other = {"tensor": 2 * chip + 1 - core}

    def at_pos(p):
        return lax.rem(p + 2 * n, n)

    nxt = {"tensor": 2 * chip_of(n, at_pos(pos + way)) + core}
    prv = {"tensor": 2 * chip_of(n, at_pos(pos - way)) + core}

    def block_row(p, c):
        return pl.multiple_of((2 * chip_of(n, at_pos(p)) + c) * rows, rows)

    def remote(src, dst, s_sem, r_sem, to):
        return pltpu.make_async_remote_copy(
            src_ref=src, dst_ref=dst, send_sem=s_sem, recv_sem=r_sem,
            device_id=to, device_id_type=MESH,
        )

    def piece_at(p, c, h):
        return normed.at[pl.ds(pl.multiple_of(block_row(p, c) + h * piece, piece), piece), :]

    def ring(s, h):
        ref = piece_at(pos - way * s, core, h)
        return remote(ref, ref, ring_s.at[s, h], ring_r.at[s, h], nxt)

    def ring_in(s, h):
        ref = piece_at(pos - way * (s + 1), core, h)
        return remote(ref, ref, ring_s.at[s, h], ring_r.at[s, h], nxt)

    def fwd(s, h):
        ref = piece_at(pos - way * s, core, h)
        return remote(ref, ref, fwd_s.at[s, h], fwd_r.at[s, h], other)

    def fwd_in(s, h):
        ref = piece_at(pos + way * s, 1 - core, h)
        return remote(ref, ref, fwd_s.at[s, h], fwd_r.at[s, h], other)

    wo_piece = wo.shape[0] // n

    def wo_copy(s, c):
        part = pl.ds(pl.multiple_of(s * wo_piece, wo_piece), wo_piece)
        return remote(wo.at[part, :], wo_v.at[c, part, :], wo_s.at[s], wo_r.at[s], other)

    kv_rows = wk.shape[0]

    def kv_slot(c, i):
        start = i * HEAD_DIM + (c * kv_rows if shared else 0)
        return wkv_v.at[pl.ds(pl.multiple_of(start, 16), kv_rows), :]

    local = [
        pltpu.make_async_copy(wk, kv_slot(core, 0), loc.at[1]),
        pltpu.make_async_copy(wv, kv_slot(core, 1), loc.at[2]),
        pltpu.make_async_copy(wq, wq_v, loc.at[0]),
    ]
    own_wo = pltpu.make_async_copy(wo, wo_v.at[core], loc.at[3])

    barrier = pltpu.get_barrier_semaphore()
    for to in (prv, other):
        pl.semaphore_signal(barrier, inc=1, device_id=to, device_id_type=MESH)

    for h in range(HALVES):
        x = tokens[h * piece : (h + 1) * piece, :].astype(F32)
        scale = lax.rsqrt(jnp.mean(x * x, axis=-1, keepdims=True) + 1e-05)
        at = pl.ds(pl.multiple_of(block_row(pos, core) + h * piece, piece), piece)
        normed[at, :] = (x * scale * gain[...]).astype(BF16)
        if h == 0:
            pl.semaphore_wait(barrier, 2)
        ring(0, h).start()
    for h in range(HALVES):
        fwd(0, h).start()
    if shared:
        kv = [
            remote(wk, kv_slot(core, 0), kv_s.at[0], kv_r.at[0], other),
            remote(wv, kv_slot(core, 1), kv_s.at[1], kv_r.at[1], other),
        ]
        for c in kv:
            c.start()
    for c in local:
        c.start()
    own_wo.start()

    def tables():
        drow = docs[...].astype(F32)
        doc_v[...] = jnp.transpose(jnp.broadcast_to(drow, (HEAD_DIM, count)))
        lane = lax.broadcasted_iota(jnp.int32, (1, HEAD_DIM), 1)
        sign = jnp.where(lane < HEAD_DIM // 2, F32(-1.0), F32(1.0))
        half = lax.rem(lane, HEAD_DIM // 2).astype(F32)
        freq = jnp.exp(half * F32(-2.0 * math.log(500000.0) / HEAD_DIM))
        tile = 128

        def one(i, carry):
            at = pl.ds(pl.multiple_of(i * tile, tile), tile)
            less = (drow < doc_v[at, 0:1]).astype(F32)
            first = jnp.sum(less, axis=1, keepdims=True)
            index = (lax.broadcasted_iota(jnp.int32, (tile, 1), 0) + i * tile).astype(F32)
            angle = (index - first) * freq
            cos_v[at, :] = jnp.cos(angle)
            sin_v[at, :] = jnp.sin(angle) * sign
            return carry

        lax.fori_loop(0, count // tile, one, 0)

    def weights_in():
        for c in local:
            c.wait()
        if shared:
            for i in range(2):
                remote(wk, kv_slot(1 - core, i), kv_s.at[i], kv_r.at[i], other).wait_recv()

    def rope(u, at):
        return u * cos_v[at, :] + pltpu.roll(u, HEAD_DIM // 2, 1) * sin_v[at, :]

    deep = 8192

    def product(starts, weights, turned):
        size = weights.shape[0] if turned else weights.shape[1]

        def one(i, acc):
            k = pl.ds(pl.multiple_of(i * deep, deep), deep)
            left = jnp.concatenate([normed[pl.ds(a, rows), k] for a in starts], axis=0)
            if turned:
                return acc + lax.dot_general(
                    left, weights[:, k], (((1,), (1,)), ((), ())), preferred_element_type=F32
                )
            return acc + jnp.dot(left, weights[k, :], preferred_element_type=F32)

        start = jnp.zeros((rows * len(starts), size), F32)
        return lax.fori_loop(0, width // deep, one, start)

    def do_queries(starts):
        raw_q = product(starts, wq_v, False)
        for i, a in enumerate(starts):
            at = pl.ds(a, rows)
            for h in range(heads):
                u = raw_q[i * rows : (i + 1) * rows, h * HEAD_DIM : (h + 1) * HEAD_DIM]
                q_v[at, h * HEAD_DIM : (h + 1) * HEAD_DIM] = rope(u, at).astype(BF16)

    def do_keys(starts):
        both = product(starts, wkv_v, True)
        for i, a in enumerate(starts):
            at = pl.ds(a, rows)
            u = both[i * rows : (i + 1) * rows, :].astype(BF16)
            k_v[at, :] = rope(u[:, :HEAD_DIM].astype(F32), at).astype(BF16)
            v_v[at, :] = u[:, HEAD_DIM:]

    def group(s):
        return [block_row(pos - way * s, core), block_row(pos + way * s, 1 - core)]

    def step(s, carry):
        wo_copy(s, core).start()
        for h in range(HALVES):
            ring_in(s, h).wait_recv()

            @pl.when(s < n - 2)
            def _():
                ring(s + 1, h).start()

            fwd(s + 1, h).start()
            if h == 0:

                @pl.when(s == 0)
                def _():
                    tables()

                @pl.when(s == 1)
                def _():
                    weights_in()
                    for t in range(2):
                        for k in range(HALVES):
                            fwd_in(t, k).wait_recv()
                    do_queries(group(0) + group(1))

                @pl.when(s > 1)
                def _():
                    for k in range(HALVES):
                        fwd_in(s, k).wait_recv()
                    do_queries(group(s))

            if h == HALVES - 1:

                @pl.when(s == 1)
                def _():
                    do_keys(group(0) + group(1))

                @pl.when(s > 1)
                def _():
                    do_keys(group(s))

        return carry

    lax.fori_loop(0, n - 1, step, 0)
    wo_copy(n - 1, core).start()
    for h in range(HALVES):
        fwd_in(n - 1, h).wait_recv()
    do_keys(group(n - 1))
    do_queries(group(n - 1))

    def sent(s, carry):
        for h in range(HALVES):
            fwd(s, h).wait_send()

            @pl.when(s < n - 1)
            def _():
                ring(s, h).wait_send()

        wo_copy(s, core).wait_send()
        return carry

    lax.fori_loop(0, n, sent, 0)
    if shared:
        for c in kv:
            c.wait_send()

    block = 256
    root = F32(1.0 / HEAD_DIM**0.5)
    swaps = []
    for i in reversed(range(count // block)):
        seen = (i + 1) * block
        span = slice(i * block, seen)
        r_idx = lax.broadcasted_iota(jnp.int32, (block, seen), 0) + i * block
        c_idx = lax.broadcasted_iota(jnp.int32, (block, seen), 1)
        visible = (c_idx <= r_idx) & (docs[:, :seen].astype(F32) == doc_v[span, 0:1])
        queries = jnp.concatenate(
            [q_v[span, h * HEAD_DIM : (h + 1) * HEAD_DIM] for h in range(heads)], axis=0
        )
        scores = lax.dot_general(
            queries, k_v[0:seen, :], (((1,), (1,)), ((), ())), preferred_element_type=F32
        ).reshape(heads, block, seen)
        scores = jnp.where(visible[None], scores * root, F32(-1e30))
        weights = jnp.exp(scores - jnp.max(scores, axis=-1, keepdims=True))
        total = jnp.sum(weights, axis=-1, keepdims=True)
        probs = (weights * (1.0 / total)).astype(BF16).reshape(heads * block, seen)
        result = jnp.dot(probs, v_v[0:seen, :], preferred_element_type=F32).astype(BF16)
        for h in range(heads):
            for j in range(block // rows):
                t = i * (block // rows) + j
                att_v[t % 2, (t // 2) * rows : (t // 2 + 1) * rows, h * HEAD_DIM : (h + 1) * HEAD_DIM] = result[
                    h * block + j * rows : h * block + (j + 1) * rows
                ]
        part = pl.ds(i * block // 2, block // 2)
        swap = remote(
            att_v.at[1 - core, part, :], att_in.at[part, :], at_s.at[i], at_r.at[i], other
        )
        swap.start()
        swaps.append(swap)
    own_wo.wait()

    def arrived(s, carry):
        wo_copy(s, 1 - core).wait_recv()
        return carry

    lax.fori_loop(0, n, arrived, 0)
    for swap in swaps:
        swap.wait()

    def part_row(p):
        return pl.multiple_of(chip_of(n, at_pos(p)) * rows, rows)

    def part_of(p, k):
        return (pl.ds(part_row(p), rows), slice(k * cols, (k + 1) * cols))

    def reduced(s, k, src):
        dst = inbox.at[s, :, k * cols : (k + 1) * cols]
        return remote(src, dst, rs_s.at[s, k], rs_r.at[s, k], nxt)

    def first_out(k):
        at, cs = part_of(pos - way, k)
        return reduced(0, k, normed.at[at, cs])

    def later_out(s, k):
        return reduced(s, k, inbox.at[s - 1, :, k * cols : (k + 1) * cols])

    thin = 1024
    for k in range(PARTS):

        def one(i, carry):
            cs = pl.ds(pl.multiple_of(k * cols + i * thin, thin), thin)
            left = jnp.concatenate([att_v[core], att_in[...]], axis=1)
            right = jnp.concatenate([wo_v[core, :, cs], wo_v[1 - core, :, cs]], axis=0)
            out = jnp.dot(left, right, preferred_element_type=F32)
            normed[0 : n * rows, cs] = out.astype(BF16)
            return carry

        lax.fori_loop(0, cols // thin, one, 0)
        first_out(k).start()

    def hop(s, carry):
        for k in range(PARTS):
            cs = slice(k * cols, (k + 1) * cols)
            reduced(s - 1, k, inbox.at[s - 1, :, cs]).wait_recv()
            at, _ = part_of(pos - way * (s + 1), k)
            both = inbox[s - 1, :, cs].astype(F32) + normed[at, cs].astype(F32)
            inbox[s - 1, :, cs] = both.astype(BF16)
            later_out(s, k).start()
        return carry

    lax.fori_loop(1, n - 1, hop, 0)
    for k in range(PARTS):
        cs = slice(k * cols, (k + 1) * cols)
        reduced(n - 2, k, inbox.at[n - 2, :, cs]).wait_recv()
        at, _ = part_of(pos, k)
        total = inbox[n - 2, :, cs].astype(F32) + normed[at, cs].astype(F32)
        total_out[:, cs] = total

    for k in range(PARTS):
        first_out(k).wait_send()

    def left(s, carry):
        for k in range(PARTS):
            later_out(s, k).wait_send()
        return carry

    lax.fori_loop(1, n - 1, left, 0)


def body(tokens, attn_gain, w_query, w_key, w_value, w_output, doc_ids):
    n = lax.axis_size("tensor") // 2
    rows, width = tokens.shape
    count = doc_ids.shape[0]
    mine = w_query.shape[1]
    heads = mine // HEAD_DIM
    levels = (HEAD_DIM // w_key.shape[1]).bit_length() - 1
    shared = levels == 1
    if not shared:
        place = lax.axis_index("tensor")
        stacked = jnp.stack([w_key, w_value])
        for bit in range(levels):
            stacked = join_cols(stacked, swapped(stacked, "tensor", bit), place, bit)
        w_key, w_value = stacked[0], stacked[1]
    vmem = pl.BlockSpec(memory_space=pltpu.VMEM)
    hbm = pl.BlockSpec(memory_space=pl.ANY)
    dma = pltpu.SemaphoreType.DMA
    total = pl.pallas_call(
        functools.partial(kernel, n, heads, shared),
        out_shape=jax.ShapeDtypeStruct((rows, width), F32),
        in_specs=[vmem, vmem, hbm, hbm, hbm, hbm, vmem],
        out_specs=vmem,
        scratch_shapes=[
            pltpu.VMEM((count, width), BF16),
            pltpu.VMEM((width, mine), BF16),
            pltpu.VMEM((2 * HEAD_DIM, width), BF16),
            pltpu.VMEM((2, mine, width), BF16),
            pltpu.VMEM((count, mine), BF16),
            pltpu.VMEM((count, HEAD_DIM), BF16),
            pltpu.VMEM((count, HEAD_DIM), BF16),
            pltpu.VMEM((2, n * rows, mine), BF16),
            pltpu.VMEM((n * rows, mine), BF16),
            pltpu.VMEM((count, HEAD_DIM), F32),
            pltpu.VMEM((count, HEAD_DIM), F32),
            pltpu.VMEM((count, HEAD_DIM), F32),
            pltpu.VMEM((n - 1, rows, width), BF16),
            dma((n - 1, HALVES)), dma((n - 1, HALVES)),
            dma((n, HALVES)), dma((n, HALVES)),
            dma((2,)), dma((2,)),
            dma((n,)), dma((n,)),
            dma((count // 128,)), dma((count // 128,)),
            dma((n - 1, PARTS)), dma((n - 1, PARTS)),
            dma((4,)),
        ],
        compiler_params=pltpu.CompilerParams(
            collective_id=0, has_side_effects=True, vmem_limit_bytes=60 * 1024 * 1024
        ),
    )(tokens, attn_gain[None, :], w_query, w_key.T, w_value.T, w_output, doc_ids[None, :])
    return (total.astype(BF16), (tokens.astype(F32) + total).astype(BF16))


def solution(mesh):
    placed = (
        P(("groups", "tensor"), None),
        P(),
        P(None, "tensor"),
        P(None, "tensor"),
        P(None, "tensor"),
        P("tensor", None),
        P("groups"),
    )
    return jax.shard_map(
        body,
        mesh=mesh,
        in_specs=placed,
        out_specs=(P(("groups", "tensor"), None), P(("groups", "tensor"), None)),
        check_vma=False,
    )
```
